32 devices in a mesh: space: 4 (over z), chaos: 8 (over y, x, core).
Axes of the slice: x: 2, y: 2, z: 4, core: 2. Of those that a mesh axis runs over, the one named last changes fastest.
Arguments:
- field: float32 [448, 8, 8, 128], P('chaos', 'space'), may hold values from -6 to 6
- modes: float32 [21, 8, 8, 128], P(None, 'space'), may hold values from -6 to 6
- send_rows: int32 [8, 64], P('chaos'), may hold values from 0 to 55, as said below
- pick: int32 [448, 41], P('chaos'), may hold values from 0 to 63
- mode_ids: int32 [448, 41], P('chaos'), may hold values from 0 to 20
- coef: float32 [448, 41], P('chaos'), may hold values from -0.15 to 0.15
Outputs:
- first: float32 [448, 8, 8, 128], P('chaos', 'space')
- second: float32 [448, 8, 8, 128], P('chaos', 'space')
The draws below stay inside these ranges and needn't reach their ends.
Inputs may be any that keep to these rules, and one draw needn't show every extreme that they name: `send_rows`: in row e, each block of 8 entries d * 8 to d * 8 + 7 holds different local terms of owner e.
All inputs are finite; a program needn't handle non-finite values.
Results may differ from the reference program's by a relative error of at most 0.000098.
Values sent between devices are 32-bit elements; how exact they have to be, the bound alone decides.
No kernel may reach another device: no remote copies, remote signals or barrier semaphores. Data moves between devices by JAX's collectives and lax.ppermute only.
A program may use at most 64 MiB of HBM per device.

```python
import jax
import jax.numpy as jnp
from jax import lax

MODES = 21
TERMS_DEV = 56
SLOTS = 41
CAP = 8
GX = 8
GY = 128
GROUPS = 8
TERMS = 448
POOL = 64
NZ = 8


def draw_send_rows(key, part):
    keys = jax.random.split(key, GROUPS * GROUPS)
    lists = jax.vmap(lambda single: jax.random.permutation(single, TERMS_DEV)[:CAP])(keys)
    return lists.reshape(GROUPS, GROUPS * CAP).astype(jnp.int32)


def place_ends(entries, own_key, least, top_value):
    dims = entries.shape
    index_at = [jax.random.randint(jax.random.fold_in(own_key, axis), (), 0, dims[axis]) for axis in range(len(dims))]
    entries = entries.at[tuple(index_at)].set(least)
    longest = dims.index(max(dims))
    index_at[longest] = (index_at[longest] + 1) % dims[longest]
    return entries.at[tuple(index_at)].set(top_value)


def block_levels(key, extent, shards, low, high):
    def one(position, blocks):
        heights = jax.random.uniform(jax.random.fold_in(jax.random.fold_in(key, 6), position), (blocks,), jnp.float32, low / len(shards), high / len(shards))
        return jnp.repeat(jnp.exp(heights), extent[position] // blocks).reshape((-1,) + (1,) * (len(extent) - position - 1))

    factor_of = one(*shards[0])
    for cut in shards[1:]:
        factor_of = factor_of * one(*cut)
    return factor_of


def normal_values(stream_key, extent, width, most, cuts=(), kind=jnp.bfloat16):
    array = width * jax.random.normal(stream_key, extent, jnp.float32)
    if cuts:
        array = array * block_levels(stream_key, extent, cuts, -0.22, 0.18)
    return jnp.clip(array, -most, most).astype(kind)


def setup_inputs(seed: int = 0) -> dict:
    key_list = jax.random.split(jax.random.key(seed), 7)
    return {
        "field": normal_values(key_list[0], (TERMS, NZ, GX, GY), 1.0, 6.0, ((0, 8), (1, 4)), jnp.float32),
        "modes": normal_values(key_list[1], (MODES, NZ, GX, GY), 1.0, 6.0, ((1, 4),), jnp.float32),
        "send_rows": draw_send_rows(jax.random.fold_in(key_list[6], 71), 0),
        "pick": place_ends(jax.random.randint(key_list[3], (TERMS, SLOTS), 0, POOL), jax.random.fold_in(key_list[3], 1), 0, POOL - 1).astype(jnp.int32),
        "mode_ids": place_ends(jax.random.randint(key_list[4], (TERMS, SLOTS), 0, MODES), jax.random.fold_in(key_list[4], 1), 0, MODES - 1).astype(jnp.int32),
        "coef": normal_values(key_list[5], (TERMS, SLOTS), 0.025, 0.15, ((0, 8),), jnp.float32),
    }


def laplace(padded):
    center = padded[:, 1:-1]
    side = jnp.pad(center, ((0, 0), (0, 0), (1, 1), (1, 1)))
    beside = padded[:, 2:] + padded[:, :-2]
    beside = beside + side[:, :, 2:, 1:-1] + side[:, :, :-2, 1:-1]
    beside = beside + side[:, :, 1:-1, 2:] + side[:, :, 1:-1, :-2]
    return 6.0 * center - beside


def reference(field, modes, send_rows, pick, mode_ids, coef):
    owner = (jnp.arange(TERMS, dtype=jnp.int32) // TERMS_DEV)[:, None]
    source = pick // CAP
    within = pick % CAP
    local_rows = send_rows[source, owner * CAP + within]
    column = (source * TERMS_DEV + local_rows).astype(jnp.int32)
    flat_modes = modes.reshape(MODES, -1)

    def apply(values):
        padded = jnp.pad(values, ((0, 0), (1, 1), (0, 0), (0, 0)))
        images = laplace(padded).reshape(TERMS, -1)

        def one_row(packed):
            cols, mds, cfs = packed
            return jnp.sum(cfs[:, None] * images[cols] * flat_modes[mds], axis=0)

        return lax.map(one_row, (column, mode_ids, coef)).reshape(values.shape)

    first = apply(field)
    second = apply(first)
    return (first, second)
```

```python
import jax
import jax.numpy as jnp
from jax import lax
from jax.sharding import PartitionSpec as P

AXES = ("space", "chaos")


def swaps(slabs, owners, first):
    partner = {}
    for left in range(first, slabs - 1, 2):
        partner[left], partner[left + 1] = left + 1, left
    pairs = []
    for s in range(slabs):
        for d in range(owners):
            other = partner[s] * owners + d if s in partner else s * owners + (d ^ 1)
            pairs.append((s * owners + d, other))
    return pairs


def inplane(values):
    side = jnp.pad(values, ((0, 0), (1, 1), (1, 1)))
    return side[:, 2:, 1:-1] + side[:, :-2, 1:-1] + side[:, 1:-1, 2:] + side[:, 1:-1, :-2]


def body(slabs, owners, field, modes, send_rows, pick, mode_ids, coef):
    space, own = lax.axis_index("space"), lax.axis_index("chaos")
    own_terms, slots = pick.shape
    count_modes = modes.shape[0]
    pool_size = send_rows.shape[1]
    cap = pool_size // owners
    chips = owners // 2
    plane = field.shape[2:]
    cells = plane[0] * plane[1]
    pairs_a, pairs_b = swaps(slabs, owners, 0), swaps(slabs, owners, 1)

    odd = space % 2 == 1
    has_a = jnp.where(odd, True, space + 1 < slabs)
    has_b = jnp.where(odd, space + 1 < slabs, space > 0)

    def split(array):
        return jnp.where(odd, array[:, 0], array[:, 1]), jnp.where(odd, array[:, 1], array[:, 0])

    def merge(near, far):
        return jnp.stack([jnp.where(odd, near, far), jnp.where(odd, far, near)], axis=1)

    order = own ^ jnp.arange(owners, dtype=jnp.int32)
    rows = jnp.take(send_rows[0].reshape(owners, cap), order, axis=0)
    place_of = ((pick // cap) ^ own) * cap + pick % cap
    place = (place_of[:, :, None] == jnp.arange(pool_size, dtype=jnp.int32)).astype(jnp.float32)
    place = place * coef[:, :, None]
    which = (mode_ids[:, :, None] == jnp.arange(count_modes, dtype=jnp.int32)).astype(jnp.float32)
    weights = jnp.einsum("isp,isk->ikp", place, which, precision=lax.Precision.HIGHEST)
    weights = weights.reshape(own_terms * count_modes, pool_size)
    mode_planes = jnp.stack(split(modes), axis=1).reshape(count_modes, 2 * cells)

    def apply(near, far):
        halo_a = lax.ppermute(near, AXES, pairs_a)
        halo_b = lax.ppermute(far, AXES, pairs_b)
        image_near = 6.0 * near - inplane(near) - far - jnp.where(has_a, halo_a, 0.0)
        image_far = 6.0 * far - inplane(far) - near - jnp.where(has_b, halo_b, 0.0)
        images = jnp.stack([image_near, image_far], axis=1)
        mine = jnp.take(images, rows[0::2].reshape(-1), axis=0).reshape(chips, cap, 2, *plane)
        others = jnp.take(images, rows[1::2].reshape(-1), axis=0).reshape(chips, cap, 2, *plane)
        others = lax.ppermute(others, "chaos", [(i, i ^ 1) for i in range(owners)])
        blocks = jnp.stack([mine, others], axis=1)
        arrived = [blocks[0]]
        for m in range(1, chips):
            arrived.append(lax.ppermute(blocks[m], "chaos", [(i, i ^ (2 * m)) for i in range(owners)]))
        pool = jnp.concatenate(arrived, axis=0).reshape(pool_size, 2 * cells)
        mixed = jnp.dot(
            weights, pool, precision=lax.Precision.HIGHEST, preferred_element_type=jnp.float32
        ).reshape(own_terms, count_modes, 2 * cells)
        result = jnp.sum(mixed * mode_planes[None], axis=1).reshape(own_terms, 2, *plane)
        return result[:, 0], result[:, 1]

    first = apply(*split(field))
    second = apply(*first)
    return merge(*first), merge(*second)


def solution(mesh):
    slabs, owners = mesh.shape["space"], mesh.shape["chaos"]

    def per_device(*args):
        return body(slabs, owners, *args)

    in_specs = (
        P("chaos", "space", None, None),
        P(None, "space", None, None),
        P("chaos", None),
        P("chaos", None),
        P("chaos", None),
        P("chaos", None),
    )
    out_specs = (P("chaos", "space", None, None), P("chaos", "space", None, None))
    return jax.shard_map(
        per_device, mesh=mesh, in_specs=in_specs, out_specs=out_specs, check_vma=False
    )
```

```python
import functools

import jax
import jax.numpy as jnp
from jax import lax
from jax.experimental import pallas as pl
from jax.experimental.pallas import tpu as pltpu
from jax.sharding import PartitionSpec as P

AXES = ("space", "chaos")
VMEM = pl.BlockSpec(memory_space=pltpu.VMEM)
SMEM = pl.BlockSpec(memory_space=pltpu.SMEM)
LIMIT = 32 * 1024 * 1024


def swaps(slabs, owners, first):
    partner = {}
    for left in range(first, slabs - 1, 2):
        partner[left], partner[left + 1] = left + 1, left
    pairs = []
    for s in range(slabs):
        for d in range(owners):
            other = partner[s] * owners + d if s in partner else s * owners + (d ^ 1)
            pairs.append((s * owners + d, other))
    return pairs


def images_kernel(parity, chips, cap, info, rows, near, far, halo_a, halo_b, out):
    own, has_a, has_b = info[0], info[1] > 0, info[2] > 0
    gx, gy = near.shape[1:]
    sub = lax.broadcasted_iota(jnp.int32, (gx, gy), 0)
    lane = lax.broadcasted_iota(jnp.int32, (gx, gy), 1)
    zero = jnp.zeros((gx, gy), jnp.float32)

    def laplace(center, other, halo):
        beside = jnp.where(sub > 0, pltpu.roll(center, 1, 0), zero)
        beside = beside + jnp.where(sub < gx - 1, pltpu.roll(center, gx - 1, 0), zero)
        beside = beside + jnp.where(lane > 0, pltpu.roll(center, 1, 1), zero)
        beside = beside + jnp.where(lane < gy - 1, pltpu.roll(center, gy - 1, 1), zero)
        return 6.0 * center - (beside + (other + halo))

    for chip in range(chips):
        start = (own ^ (2 * chip + parity)) * cap
        for c in range(cap):
            term = rows[0, start + c]
            a, b = near[term], far[term]
            ha = jnp.where(has_a, halo_a[term], zero)
            hb = jnp.where(has_b, halo_b[term], zero)
            base = chip * 2 * gx * cap + c
            out[pl.ds(base, gx, stride=cap), :] = laplace(a, b, ha)
            out[pl.ds(base + gx * cap, gx, stride=cap), :] = laplace(b, a, hb)


def images(parity, chips, cap, info, rows, near, far, halo_a, halo_b):
    gx, gy = near.shape[1:]
    out = pl.pallas_call(
        functools.partial(images_kernel, parity, chips, cap),
        out_shape=jax.ShapeDtypeStruct((chips * 2 * gx * cap, gy), jnp.float32),
        in_specs=[SMEM, SMEM, VMEM, VMEM, VMEM, VMEM],
        out_specs=VMEM,
        compiler_params=pltpu.CompilerParams(vmem_limit_bytes=LIMIT),
        cost_estimate=pl.CostEstimate(flops=chips * 2 * gx * cap * gy * 8, bytes_accessed=1 << 20, transcendentals=0),
        name=f"images_{parity}",
    )(info, rows, near, far, halo_a, halo_b)
    return out.reshape(chips, 2, gx, cap, gy)


def product_kernel(plane, count_modes, weights, modes, *rest):
    blocks, out = rest[:-1], rest[-1]
    gx, gy = modes.shape[1:]
    own_terms = weights.shape[0] // count_modes

    def column(g):
        parts = [block[half, plane, g] for block in blocks for half in range(2)]
        full = jnp.concatenate(parts, axis=0)
        high = full.astype(jnp.bfloat16)
        low = (full - high.astype(jnp.float32)).astype(jnp.bfloat16)
        return jnp.concatenate([high, low, high], axis=0)

    for g in range(0, gx, 2):
        pool = jnp.concatenate([column(g), column(g + 1)], axis=1)
        mixed = jnp.dot(weights[...], pool, preferred_element_type=jnp.float32)
        for side in range(2):
            total = jnp.zeros((own_terms, gy), jnp.float32)
            for k in range(count_modes):
                part = mixed[k * own_terms : (k + 1) * own_terms, side * gy : (side + 1) * gy]
                total = total + part * modes[k, pl.ds(g + side, 1), :]
            out[pl.ds(g + side, own_terms, stride=gx), :] = total


def product(plane, weights, modes, blocks):
    count_modes, gx, gy = modes.shape
    own_terms = weights.shape[0] // count_modes
    out = pl.pallas_call(
        functools.partial(product_kernel, plane, count_modes),
        out_shape=jax.ShapeDtypeStruct((own_terms * gx, gy), jnp.float32),
        in_specs=[VMEM] * (2 + len(blocks)),
        out_specs=VMEM,
        compiler_params=pltpu.CompilerParams(vmem_limit_bytes=LIMIT),
        cost_estimate=pl.CostEstimate(
            flops=2 * weights.shape[0] * weights.shape[1] * gx * gy, bytes_accessed=1 << 20, transcendentals=0
        ),
        name=f"product_{plane}",
    )(weights, modes, *blocks)
    return out.reshape(own_terms, gx, gy)


def body(slabs, owners, field, modes, send_rows, pick, mode_ids, coef):
    space, own = lax.axis_index("space"), lax.axis_index("chaos")
    own_terms = pick.shape[0]
    count_modes = modes.shape[0]
    pool_size = send_rows.shape[1]
    cap = pool_size // owners
    chips = owners // 2
    pairs_a, pairs_b = swaps(slabs, owners, 0), swaps(slabs, owners, 1)

    odd = space % 2 == 1
    near_at = jnp.where(odd, 0, 1)
    has_a = jnp.where(odd, True, space + 1 < slabs)
    has_b = jnp.where(odd, space + 1 < slabs, space > 0)
    info = jnp.stack([own, has_a.astype(jnp.int32), has_b.astype(jnp.int32)]).astype(jnp.int32)

    def split(array):
        return (
            lax.dynamic_index_in_dim(array, near_at, 1, keepdims=False),
            lax.dynamic_index_in_dim(array, 1 - near_at, 1, keepdims=False),
        )

    def merge(near, far):
        return jnp.stack([jnp.where(odd, near, far), jnp.where(odd, far, near)], axis=1)

    place_of = ((pick // cap) ^ own) * cap + pick % cap
    place = (place_of[:, :, None] == jnp.arange(pool_size, dtype=jnp.int32)).astype(jnp.float32)
    place = place * coef[:, :, None]
    which = (mode_ids[:, :, None] == jnp.arange(count_modes, dtype=jnp.int32)).astype(jnp.float32)
    weights = jnp.einsum("isp,isk->kip", place, which, precision=lax.Precision.HIGHEST)
    weights = weights.reshape(count_modes * own_terms, pool_size)
    high = lax.reduce_precision(weights, 8, 7)
    weights = jnp.concatenate([high, high, weights - high], axis=1).astype(jnp.bfloat16)
    mode_planes = split(modes)

    def apply(near, far):
        halo_a = lax.ppermute(near, AXES, pairs_a)
        halo_b = lax.ppermute(far, AXES, pairs_b)
        inputs = (info, send_rows, near, far, halo_a, halo_b)
        others = images(1, chips, cap, *inputs)
        others = lax.ppermute(others, "chaos", [(i, i ^ 1) for i in range(owners)])
        mine = images(0, chips, cap, *inputs)
        blocks = [jnp.stack([mine[m], others[m]]) for m in range(chips)]
        for m in range(1, chips):
            blocks[m] = lax.ppermute(blocks[m], "chaos", [(i, i ^ (2 * m)) for i in range(owners)])
        return tuple(product(plane, weights, mode_planes[plane], blocks) for plane in range(2))

    first = apply(*split(field))
    second = apply(*first)
    return merge(*first), merge(*second)


def solution(mesh):
    slabs, owners = mesh.shape["space"], mesh.shape["chaos"]

    def per_device(*args):
        return body(slabs, owners, *args)

    in_specs = (
        P("chaos", "space", None, None),
        P(None, "space", None, None),
        P("chaos", None),
        P("chaos", None),
        P("chaos", None),
        P("chaos", None),
    )
    out_specs = (P("chaos", "space", None, None), P("chaos", "space", None, None))
    return jax.shard_map(
        per_device, mesh=mesh, in_specs=in_specs, out_specs=out_specs, check_vma=False
    )
```

```python
import functools

import jax
import jax.numpy as jnp
from jax import lax
from jax.experimental import pallas as pl
from jax.experimental.pallas import tpu as pltpu
from jax.sharding import PartitionSpec as P

AXES = ("space", "chaos")
VMEM = pl.BlockSpec(memory_space=pltpu.VMEM)
ANY = pl.BlockSpec(memory_space=pl.ANY)
SMEM = pl.BlockSpec(memory_space=pltpu.SMEM)
LIMIT = 32 * 1024 * 1024


def swaps(slabs, owners, first):
    partner = {}
    for left in range(first, slabs - 1, 2):
        partner[left], partner[left + 1] = left + 1, left
    pairs = []
    for s in range(slabs):
        for d in range(owners):
            other = partner[s] * owners + d if s in partner else s * owners + (d ^ 1)
            pairs.append((s * owners + d, other))
    return pairs


def images_kernel(plane, parities, chips, cap, rows, flags, center, other, halo, *rest):
    outs = rest[-len(parities) :]
    gx, gy = center.shape[1:]
    sub = lax.broadcasted_iota(jnp.int32, (gx, gy), 0)
    lane = lax.broadcasted_iota(jnp.int32, (gx, gy), 1)
    zero = jnp.zeros((gx, gy), jnp.float32)
    inside = flags[pl.ds(plane, 1), :] > 0
    terms = rows[...]

    def laplace(term):
        middle = center[term]
        beside = jnp.where(sub > 0, pltpu.roll(middle, 1, 0), zero)
        beside = beside + jnp.where(sub < gx - 1, pltpu.roll(middle, gx - 1, 0), zero)
        beside = beside + jnp.where(lane > 0, pltpu.roll(middle, 1, 1), zero)
        beside = beside + jnp.where(lane < gy - 1, pltpu.roll(middle, gy - 1, 1), zero)
        beside = beside + (other[term] + jnp.where(inside, halo[term], zero))
        return 6.0 * middle - beside

    for parity, out in zip(parities, outs):
        for chip in range(chips):
            at = (2 * chip + parity) * cap
            made = [laplace(terms[0, at + c]) for c in range(cap)]
            for c in range(cap):
                out[pl.ds((chip * 2 + plane) * gx * cap + c, gx, stride=cap), :] = made[c]


def images(plane, parities, chips, cap, rows, flags, center, other, halo, partial=()):
    gx, gy = center.shape[1:]
    out = jax.ShapeDtypeStruct((chips * 2 * gx * cap, gy), jnp.float32)
    return pl.pallas_call(
        functools.partial(images_kernel, plane, parities, chips, cap),
        out_shape=[out] * len(parities),
        in_specs=[VMEM] * (5 + len(partial)),
        out_specs=[VMEM] * len(parities),
        input_output_aliases={5 + i: i for i in range(len(partial))},
        compiler_params=pltpu.CompilerParams(vmem_limit_bytes=LIMIT),
        cost_estimate=pl.CostEstimate(
            flops=len(parities) * chips * gx * cap * gy * 8, bytes_accessed=1 << 19, transcendentals=0
        ),
        name=f"images_{plane}_{len(parities)}_{parities[0]}",
    )(rows, flags, center, other, halo, *partial)


def product_kernel(plane, count_modes, order, weights, modes, *rest):
    blocks, out = [rest[order.index(m)] for m in range(len(order))], rest[-1]
    gx, gy = modes.shape[1:]
    own_terms = weights.shape[0] // count_modes

    def column(g):
        parts = [block[half, plane, g] for block in blocks for half in range(2)]
        full = jnp.concatenate(parts, axis=0)
        high = full.astype(jnp.bfloat16)
        low = (full - high.astype(jnp.float32)).astype(jnp.bfloat16)
        return jnp.concatenate([high, low, high], axis=0)

    for g in range(0, gx, 2):
        pool = jnp.concatenate([column(g), column(g + 1)], axis=1)
        mixed = jnp.dot(weights[...], pool, preferred_element_type=jnp.float32)
        for side in range(2):
            total = jnp.zeros((own_terms, gy), jnp.float32)
            for k in range(count_modes):
                part = mixed[k * own_terms : (k + 1) * own_terms, side * gy : (side + 1) * gy]
                total = total + part * modes[k, pl.ds(g + side, 1), :]
            out[pl.ds(g + side, own_terms, stride=gx), :] = total


def product(plane, weights, modes, blocks, order, after=()):
    count_modes, gx, gy = modes.shape
    own_terms = weights.shape[0] // count_modes
    out = pl.pallas_call(
        functools.partial(product_kernel, plane, count_modes, order),
        out_shape=jax.ShapeDtypeStruct((own_terms * gx, gy), jnp.float32),
        in_specs=[VMEM] * (2 + len(blocks)) + [ANY] * len(after),
        out_specs=VMEM,
        compiler_params=pltpu.CompilerParams(vmem_limit_bytes=LIMIT),
        cost_estimate=pl.CostEstimate(
            flops=2 * weights.shape[0] * weights.shape[1] * gx * gy, bytes_accessed=1 << 20, transcendentals=0
        ),
        name=f"product_{plane}",
    )(weights, modes, *[blocks[m] for m in order], *after)
    return out.reshape(own_terms, gx, gy)


def body(slabs, owners, field, modes, send_rows, pick, mode_ids, coef):
    space, own = lax.axis_index("space"), lax.axis_index("chaos")
    own_terms = pick.shape[0]
    count_modes = modes.shape[0]
    pool_size = send_rows.shape[1]
    cap = pool_size // owners
    chips = owners // 2
    pairs_a, pairs_b = swaps(slabs, owners, 0), swaps(slabs, owners, 1)

    odd = space % 2 == 1
    near_at = jnp.where(odd, 0, 1)
    has_a = jnp.where(odd, True, space + 1 < slabs)
    has_b = jnp.where(odd, space + 1 < slabs, space > 0)
    flags = jnp.broadcast_to(jnp.stack([has_a, has_b]).astype(jnp.int32)[:, None], (2, field.shape[3]))

    def split(array):
        return (
            lax.dynamic_index_in_dim(array, near_at, 1, keepdims=False),
            lax.dynamic_index_in_dim(array, 1 - near_at, 1, keepdims=False),
        )

    def merge(near, far):
        return jnp.stack([jnp.where(odd, near, far), jnp.where(odd, far, near)], axis=1)

    rows = jnp.take(send_rows.reshape(owners, cap), own ^ jnp.arange(owners), axis=0).reshape(1, pool_size)
    place_of = ((pick // cap) ^ own) * cap + pick % cap
    place = (place_of[:, :, None] == jnp.arange(pool_size, dtype=jnp.int32)).astype(jnp.float32)
    place = place * coef[:, :, None]
    which = (mode_ids[:, :, None] == jnp.arange(count_modes, dtype=jnp.int32)).astype(jnp.float32)
    weights = jnp.einsum("isp,isk->kip", place, which, precision=lax.Precision.HIGHEST)
    weights = weights.reshape(count_modes * own_terms, pool_size)
    high = lax.reduce_precision(weights, 8, 7)
    weights = jnp.concatenate([high, high, weights - high], axis=1).astype(jnp.bfloat16)
    mode_planes = split(modes)

    def apply(near, far):
        halo_a = lax.ppermute(near, AXES, pairs_a)
        halo_b = lax.ppermute(far, AXES, pairs_b)
        first_plane = images(0, (1, 0), chips, cap, rows, flags, near, far, halo_a)
        (others,) = images(1, (1,), chips, cap, rows, flags, far, near, halo_b, first_plane[:1])
        shape = (chips, 2, field.shape[2], cap, field.shape[3])
        others = lax.ppermute(others.reshape(shape), "chaos", [(i, i ^ 1) for i in range(owners)])
        (mine,) = images(1, (0,), chips, cap, rows, flags, far, near, halo_b, first_plane[1:])
        mine = mine.reshape(shape)
        blocks = [jnp.stack([mine[m], others[m]]) for m in range(chips)]
        order = sorted(range(chips), key=lambda m: (m > 0, -bin(m).count("1"), m))
        for m in order[1:]:
            blocks[m] = lax.ppermute(blocks[m], "chaos", [(i, i ^ (2 * m)) for i in range(owners)])
        return tuple(product(plane, weights, mode_planes[plane], blocks, order) for plane in range(2))

    first = apply(*split(field))
    second = apply(*first)
    return merge(*first), merge(*second)


def solution(mesh):
    slabs, owners = mesh.shape["space"], mesh.shape["chaos"]

    def per_device(*args):
        return body(slabs, owners, *args)

    in_specs = (
        P("chaos", "space", None, None),
        P(None, "space", None, None),
        P("chaos", None),
        P("chaos", None),
        P("chaos", None),
        P("chaos", None),
    )
    out_specs = (P("chaos", "space", None, None), P("chaos", "space", None, None))
    return jax.shard_map(
        per_device, mesh=mesh, in_specs=in_specs, out_specs=out_specs, check_vma=False
    )
```

```python
import functools

import jax
import jax.numpy as jnp
from jax import lax
from jax.experimental import pallas as pl
from jax.experimental.pallas import tpu as pltpu
from jax.sharding import PartitionSpec as P

AXES = ("space", "chaos")
ANY = pl.BlockSpec(memory_space=pl.ANY)
VMEM = pl.BlockSpec(memory_space=pltpu.VMEM)
BATCH = 8
PARAMS = pltpu.CompilerParams(vmem_limit_bytes=32 * 1024 * 1024)


def cost(flops):
    return pl.CostEstimate(flops=flops, bytes_accessed=1 << 20, transcendentals=0)


def slab_pairs(slabs, owners):
    pairs = []
    for s in range(slabs):
        for d in range(owners):
            beside = s + 1 if d % 2 else s - 1
            other = beside * owners + (d ^ 1) if 0 <= beside < slabs else s * owners + (d ^ 2 if owners > 2 else d)
            pairs.append((s * owners + d, other))
    return pairs


def local_kernel(center_own, center_beside, other_own, other_beside, *rest):
    gx, gy = center_own.shape[1:]
    sub = lax.broadcasted_iota(jnp.int32, (gx, gy), 0)
    lane = lax.broadcasted_iota(jnp.int32, (gx, gy), 1)
    zero = jnp.zeros((gx, gy), jnp.float32)

    def laplace(middle, other):
        beside = jnp.where(sub > 0, pltpu.roll(middle, 1, 0), zero)
        beside = beside + jnp.where(sub < gx - 1, pltpu.roll(middle, gx - 1, 0), zero)
        beside = beside + jnp.where(lane > 0, pltpu.roll(middle, 1, 1), zero)
        beside = beside + jnp.where(lane < gy - 1, pltpu.roll(middle, gy - 1, 1), zero)
        return 6.0 * middle - (beside + other)

    for center, other, out in zip((center_own, center_beside), (other_own, other_beside), rest[-2:]):
        for start in range(0, center.shape[0], BATCH):
            terms = range(start, min(start + BATCH, center.shape[0]))
            made = [laplace(center[term], other[term]) for term in terms]
            for term, value in zip(terms, made):
                out[term] = value


def local(centers, others, after=()):
    out = jax.ShapeDtypeStruct(centers[0].shape, jnp.float32)
    return pl.pallas_call(
        local_kernel,
        out_shape=[out, out],
        in_specs=[VMEM] * 4 + [ANY] * len(after),
        out_specs=[VMEM] * 2,
        compiler_params=PARAMS,
        cost_estimate=cost(out.size * 16),
        name="local",
    )(*centers, *others, *after)


def images_kernel(a, blocks, chips, cap, rows, flag, partial, halo, *rest):
    outs = rest[-len(chips) :]
    gx, gy = partial.shape[1:]
    zero = jnp.zeros((gx, gy), jnp.float32)
    inside = flag[...] > 0
    terms = rows[...]
    for m, out in zip(chips, outs):
        for n in range(4 * m, 4 * m + 4):
            if blocks[n][0] == a:
                picked = [terms[0, blocks[n][1] * cap + c] for c in range(cap)]
                made = [partial[term] - jnp.where(inside, halo[term], zero) for term in picked]
                for c in range(cap):
                    out[pl.ds((n - 4 * m) * gx * cap + c, gx, stride=cap), :] = made[c]


def images(a, blocks, chips, cap, rows, flag, partial, halos, begun=(), after=()):
    gx, gy = halos[a].shape[1:]
    out = jax.ShapeDtypeStruct((4 * gx * cap, gy), jnp.float32)
    return pl.pallas_call(
        functools.partial(images_kernel, a, blocks, chips, cap),
        out_shape=[out] * len(chips),
        in_specs=[VMEM] * (4 + len(begun)) + [ANY] * len(after),
        out_specs=[VMEM] * len(chips),
        input_output_aliases={4 + i: i for i in range(len(begun))},
        compiler_params=PARAMS,
        cost_estimate=cost(out.size * len(chips)),
        name=f"images_{a}_{chips[0]}",
    )(rows[a], flag, partial[a], halos[a], *begun, *after)


def product_kernel(b, cap, count, weights, modes, *rest):
    arrays, out = rest[:count], rest[-1]
    halves = weights[...].astype(jnp.bfloat16)
    both = jnp.concatenate([halves, halves], axis=1)
    count_modes, gx, gy = modes.shape
    own_terms = weights.shape[0] // count_modes

    def column(g):
        starts = [((b * 2 + (a ^ b)) * gx + g) * cap for a in range(2)]
        full = jnp.concatenate([array[start : start + cap, :] for array in arrays for start in starts], axis=0)
        high = full.astype(jnp.bfloat16)
        low = (full - high.astype(jnp.float32)).astype(jnp.bfloat16)
        return jnp.concatenate([high, high, low, low], axis=0)

    for g in range(0, gx, 2):
        pool = jnp.concatenate([column(g), column(g + 1)], axis=1)
        mixed = jnp.dot(both, pool, preferred_element_type=jnp.float32)
        for side in range(2):
            total = jnp.zeros((own_terms, gy), jnp.float32)
            for k in range(count_modes):
                part = mixed[k * own_terms : (k + 1) * own_terms, side * gy : (side + 1) * gy]
                total = total + part * modes[k, pl.ds(g + side, 1), :]
            out[pl.ds(g + side, own_terms, stride=gx), :] = total


def product(b, cap, weights, modes, arrays, after=()):
    count_modes, gx, gy = modes.shape
    own_terms = weights.shape[0] // count_modes
    out = pl.pallas_call(
        functools.partial(product_kernel, b, cap, len(arrays)),
        out_shape=jax.ShapeDtypeStruct((own_terms * gx, gy), jnp.float32),
        in_specs=[VMEM] * (2 + len(arrays)) + [ANY] * len(after),
        out_specs=VMEM,
        compiler_params=PARAMS,
        cost_estimate=cost(4 * weights.shape[0] * weights.shape[1] * gx * gy),
        name=f"product_{b}",
    )(weights, modes, *arrays, *after)
    return out.reshape(own_terms, gx, gy)


def write_kernel(here, there, out, *rest):
    sems = rest[-1]
    core = lax.rem(lax.axis_index("chaos"), 2)
    copies = [
        pltpu.make_async_copy(here, out.at[:, core], sems.at[0]),
        pltpu.make_async_copy(there, out.at[:, 1 - core], sems.at[1]),
    ]
    for copy in copies:
        copy.start()
    for token in rest[:-1]:
        token[...] = jnp.zeros_like(token)
    for copy in copies:
        copy.wait()


def write(here, there, token):
    terms, gx, gy = here.shape
    return pl.pallas_call(
        write_kernel,
        out_shape=[jax.ShapeDtypeStruct((terms, 2, gx, gy), jnp.float32)]
        + [jax.ShapeDtypeStruct((gx, gy), jnp.float32)] * token,
        in_specs=[VMEM] * 2,
        out_specs=[ANY] + [VMEM] * token,
        scratch_shapes=[pltpu.SemaphoreType.DMA((2,))],
        compiler_params=PARAMS,
        name="write",
    )(here, there)


def body(slabs, owners, field, modes, send_rows, pick, mode_ids, coef):
    space, own = lax.axis_index("space"), lax.axis_index("chaos")
    core = own % 2
    own_terms = pick.shape[0]
    count_modes = modes.shape[0]
    pool_size = send_rows.shape[1]
    cap = pool_size // owners
    chips = owners // 2
    to_slab = slab_pairs(slabs, owners)

    def across(array):
        return lax.ppermute(array, "chaos", [(i, i ^ 1) for i in range(owners)])

    def plane(array, at):
        return lax.dynamic_index_in_dim(array, at, 1, keepdims=False)

    here, there = plane(field, core), plane(field, 1 - core)
    here_beside = across(there)
    send_rows, pick, mode_ids, coef, other, here_beside = lax.optimization_barrier(
        (send_rows, pick, mode_ids, coef, here, here_beside)
    )
    rows_beside, there_beside = across(send_rows), across(other)

    inside = jnp.where(core == 0, space > 0, space + 1 < slabs)
    flag = jnp.broadcast_to(inside.astype(jnp.int32), (1, field.shape[3]))

    def from_own(listed, index):
        for bit in range(owners.bit_length() - 1):
            size = cap << bit
            parts = [listed[:, start : start + size] for start in range(0, pool_size, size)]
            turned = jnp.concatenate([parts[n ^ 1] for n in range(len(parts))], axis=1)
            listed = jnp.where((index >> bit) & 1 == 1, turned, listed)
        return listed

    rows = from_own(send_rows, own), from_own(rows_beside, own ^ 1)
    blocks = tuple((a, 2 * m + (b ^ a)) for m in range(chips) for b in range(2) for a in range(2))

    entry = ((pick // cap) ^ own) * cap + pick % cap
    place = (entry[:, :, None] == jnp.arange(pool_size, dtype=jnp.int32)).astype(jnp.float32)
    place = place * coef[:, :, None]
    which = (mode_ids[:, :, None] == jnp.arange(count_modes, dtype=jnp.int32)).astype(jnp.float32)
    weights = jnp.einsum("isp,isk->kip", place, which, precision=lax.Precision.HIGHEST)
    weights = weights.reshape(count_modes * own_terms, pool_size)

    high = lax.reduce_precision(weights, 8, 7)
    weights = jnp.concatenate([high, weights - high], axis=1)
    weights = weights.astype(jnp.bfloat16), across(weights)
    mode_plane = plane(modes, core)

    order = sorted(range(1, chips), key=lambda m: (-bin(m).count("1"), m))

    def exchange(centers, others):
        halos = [lax.ppermute(center, AXES, to_slab) for center in centers]
        inputs = (cap, rows, flag, local(centers, others, halos[:1]), halos[::-1])
        begun = images(1, blocks, (*order, 0), *inputs)
        sent = images(0, blocks, order, *inputs, begun[:-1])
        (kept,) = images(0, blocks, (0,), *inputs, begun[-1:], sent[-1:])
        arrays = {m: lax.ppermute(x, "chaos", [(i, i ^ (2 * m)) for i in range(owners)]) for m, x in zip(order, sent)}
        return [kept, *(arrays[m] for m in range(1, chips))]

    pool = exchange((here, here_beside), (there, there_beside))
    own_first = product(0, cap, weights[0], mode_plane, pool)
    first = own_first, product(1, cap, weights[1], mode_plane, pool, (own_first,))
    beside = [across(x) for x in first]
    out, token = write(own_first, beside[1], True)
    pool = exchange(first, beside[::-1])
    theirs = across(product(1, cap, weights[1], mode_plane, pool, (token,)))
    mine = product(0, cap, weights[0], mode_plane, pool)
    return out, *write(mine, theirs, False)


def solution(mesh):
    slabs, owners = mesh.shape["space"], mesh.shape["chaos"]

    def per_device(*args):
        return body(slabs, owners, *args)

    in_specs = (
        P("chaos", "space", None, None),
        P(None, "space", None, None),
        P("chaos", None),
        P("chaos", None),
        P("chaos", None),
        P("chaos", None),
    )
    out_specs = (P("chaos", "space", None, None), P("chaos", "space", None, None))
    return jax.shard_map(
        per_device, mesh=mesh, in_specs=in_specs, out_specs=out_specs, check_vma=False
    )
```

```python
import functools

import jax
import jax.numpy as jnp
from jax import lax
from jax.experimental import pallas as pl
from jax.experimental.pallas import tpu as pltpu
from jax.sharding import PartitionSpec as P

AXES = ("space", "chaos")
ANY = pl.BlockSpec(memory_space=pl.ANY)
VMEM = pl.BlockSpec(memory_space=pltpu.VMEM)
BATCH = 8
PARAMS = pltpu.CompilerParams(vmem_limit_bytes=32 * 1024 * 1024)


def cost(flops):
    return pl.CostEstimate(flops=flops, bytes_accessed=1 << 20, transcendentals=0)


def slab_pairs(slabs, owners):
    pairs = []
    for s in range(slabs):
        for d in range(owners):
            beside = s + 1 if d % 2 else s - 1
            other = beside * owners + (d ^ 1) if 0 <= beside < slabs else s * owners + (d ^ 2 if owners > 2 else d)
            pairs.append((s * owners + d, other))
    return pairs


def local_kernel(center_own, center_beside, other_own, other_beside, *rest):
    gx, gy = center_own.shape[1:]
    sub = lax.broadcasted_iota(jnp.int32, (gx, gy), 0)
    lane = lax.broadcasted_iota(jnp.int32, (gx, gy), 1)
    zero = jnp.zeros((gx, gy), jnp.float32)

    def laplace(middle, other):
        beside = jnp.where(sub > 0, pltpu.roll(middle, 1, 0), zero)
        beside = beside + jnp.where(sub < gx - 1, pltpu.roll(middle, gx - 1, 0), zero)
        beside = beside + jnp.where(lane > 0, pltpu.roll(middle, 1, 1), zero)
        beside = beside + jnp.where(lane < gy - 1, pltpu.roll(middle, gy - 1, 1), zero)
        return 6.0 * middle - (beside + other)

    for center, other, out in zip((center_own, center_beside), (other_own, other_beside), rest[-2:]):
        for start in range(0, center.shape[0], BATCH):
            terms = range(start, min(start + BATCH, center.shape[0]))
            made = [laplace(center[term], other[term]) for term in terms]
            for term, value in zip(terms, made):
                out[term] = value


def local(centers, others, after=()):
    out = jax.ShapeDtypeStruct(centers[0].shape, jnp.float32)
    return pl.pallas_call(
        local_kernel,
        out_shape=[out, out],
        in_specs=[VMEM] * 4 + [ANY] * len(after),
        out_specs=[VMEM] * 2,
        compiler_params=PARAMS,
        cost_estimate=cost(out.size * 16),
        name="local",
    )(*centers, *others, *after)


def images_kernel(a, whole, chips, cap, rows, flag, partial, halo, *rest):
    outs = rest[-len(chips) :]
    gx, gy = partial.shape[1:]
    zero = jnp.zeros((gx, gy), jnp.float32)
    inside = flag[...] > 0
    terms = rows[...]
    for m, out in zip(chips, outs):
        for b in range(2):
            picked = [terms[0, (2 * m + b) * cap + c] for c in range(cap)]
            made = [partial[term] - jnp.where(inside, halo[term], zero) for term in picked]
            for c in range(cap):
                out[pl.ds((2 * b + a if whole else b) * gx * cap + c, gx, stride=cap), :] = made[c]


def images(a, whole, chips, cap, rows, flag, partial, halos, begun=(), after=()):
    gx, gy = partial[a].shape[1:]
    out = jax.ShapeDtypeStruct(((4 if whole else 2) * gx * cap, gy), jnp.float32)
    return pl.pallas_call(
        functools.partial(images_kernel, a, whole, chips, cap),
        out_shape=[out] * len(chips),
        in_specs=[VMEM] * (4 + len(begun)) + [ANY] * len(after),
        out_specs=[VMEM] * len(chips),
        input_output_aliases={4 + i: i for i in range(len(begun))},
        compiler_params=PARAMS,
        cost_estimate=cost(2 * gx * cap * gy * len(chips)),
        name=f"images_{a}_{chips[0]}",
    )(rows[a], flag, partial[a], halos[a], *begun, *after)


def halves_of(full):
    high = full.astype(jnp.bfloat16)
    return high, (full - high.astype(jnp.float32)).astype(jnp.bfloat16)


def early_kernel(cap, orders, *rest):
    arrays, (high, low) = rest[:-2], rest[-2:]
    gx = arrays[0].shape[0] // (2 * cap)
    count = len(arrays) * cap
    for b in range(2):
        for g in range(gx):
            n = b * gx + g
            full = jnp.concatenate([arrays[at][n * cap : (n + 1) * cap, :] for at in orders[b]], axis=0)
            high[n * count : (n + 1) * count, :], low[n * count : (n + 1) * count, :] = halves_of(full)


def early(cap, orders, arrays):
    rows, gy = arrays[0].shape
    out = jax.ShapeDtypeStruct((rows * len(arrays), gy), jnp.bfloat16)
    return pl.pallas_call(
        functools.partial(early_kernel, cap, orders),
        out_shape=[out, out],
        in_specs=[VMEM] * len(arrays),
        out_specs=[VMEM] * 2,
        compiler_params=PARAMS,
        cost_estimate=cost(1000),
        name="early",
    )(*arrays)


def product_kernel(b, cap, order, weights, modes, *rest):
    out = rest[-1]
    halves = weights[...].astype(jnp.bfloat16)
    both = jnp.concatenate([halves, halves], axis=1)
    count_modes, gx, gy = modes.shape
    own_terms = weights.shape[0] // count_modes
    count = len(order) * cap

    def blocks(arrays, n):
        return jnp.concatenate([arrays[at][n * cap : (n + 1) * cap, :] for at in order], axis=0)

    def column(g):
        if rest[0].dtype == jnp.bfloat16:
            n = b * gx + g
            late = halves_of(blocks(rest[2:], n))
            pairs = [(own, other[n * count : (n + 1) * count, :]) for own, other in zip(late, rest[:2])]
        else:
            owned = [halves_of(blocks(rest, (2 * b + a) * gx + g)) for a in range(2)]
            pairs = list(zip(*owned))
        parts = [part for pair in pairs for part in 2 * (pair[::-1] if b else pair)]
        return jnp.concatenate(parts, axis=0)

    for g in range(0, gx, 2):
        pool = jnp.concatenate([column(g), column(g + 1)], axis=1)
        mixed = jnp.dot(both, pool, preferred_element_type=jnp.float32)
        for side in range(2):
            total = jnp.zeros((own_terms, gy), jnp.float32)
            for k in range(count_modes):
                part = mixed[k * own_terms : (k + 1) * own_terms, side * gy : (side + 1) * gy]
                total = total + part * modes[k, pl.ds(g + side, 1), :]
            out[pl.ds(g + side, own_terms, stride=gx), :] = total


def product(b, cap, orders, weights, modes, pool, after=()):
    count_modes, gx, gy = modes.shape
    own_terms = weights.shape[0] // count_modes
    out = pl.pallas_call(
        functools.partial(product_kernel, b, cap, orders[b]),
        out_shape=jax.ShapeDtypeStruct((own_terms * gx, gy), jnp.float32),
        in_specs=[VMEM] * (2 + len(pool)) + [ANY] * len(after),
        out_specs=VMEM,
        compiler_params=PARAMS,
        cost_estimate=cost(4 * weights.shape[0] * weights.shape[1] * gx * gy),
        name=f"product_{b}",
    )(weights, modes, *pool, *after)
    return out.reshape(own_terms, gx, gy)


def write_kernel(here, there, out, *rest):
    sems = rest[-1]
    core = lax.rem(lax.axis_index("chaos"), 2)
    copies = [
        pltpu.make_async_copy(here, out.at[:, core], sems.at[0]),
        pltpu.make_async_copy(there, out.at[:, 1 - core], sems.at[1]),
    ]
    for copy in copies:
        copy.start()
    for token in rest[:-1]:
        token[...] = jnp.zeros_like(token)
    for copy in copies:
        copy.wait()


def write(here, there, token):
    terms, gx, gy = here.shape
    return pl.pallas_call(
        write_kernel,
        out_shape=[jax.ShapeDtypeStruct((terms, 2, gx, gy), jnp.float32)]
        + [jax.ShapeDtypeStruct((gx, gy), jnp.float32)] * token,
        in_specs=[VMEM] * 2,
        out_specs=[ANY] + [VMEM] * token,
        scratch_shapes=[pltpu.SemaphoreType.DMA((2,))],
        compiler_params=PARAMS,
        name="write",
    )(here, there)


def from_own_kernel(cap, listed, out):
    own = lax.axis_index("chaos")
    length, width = listed.shape[1], out.shape[1]
    row = listed[...]
    if width > length:
        row = jnp.concatenate([row, jnp.zeros((1, width - length), row.dtype)], axis=1)
    lane = lax.broadcasted_iota(jnp.int32, row.shape, 1)
    size = cap
    while size < length:
        turned = jnp.where(lane & size > 0, pltpu.roll(row, size, 1), pltpu.roll(row, width - size, 1))
        row = jnp.where((own & (size // cap)) > 0, turned, row)
        size *= 2
    chip = lane // (2 * cap)
    turned = jnp.where(chip % 2 == 1, pltpu.roll(row, width - 2 * cap, 1), pltpu.roll(row, 2 * cap, 1))
    moved = (chip > 0) & (chip < length // (2 * cap) // 2 * 2 - 1) & (own % 2 == 1)
    out[...] = jnp.where(moved, turned, row)


def from_own(cap, listed):
    width = -(-listed.shape[1] // 128) * 128
    return pl.pallas_call(
        functools.partial(from_own_kernel, cap),
        out_shape=jax.ShapeDtypeStruct((1, width), listed.dtype),
        in_specs=[VMEM],
        out_specs=VMEM,
        compiler_params=PARAMS,
        cost_estimate=cost(20_000_000_000),
        name="from_own",
    )(listed)


def body(slabs, owners, field, modes, send_rows, pick, mode_ids, coef):
    space, own = lax.axis_index("space"), lax.axis_index("chaos")
    core = own % 2
    own_terms = pick.shape[0]
    count_modes = modes.shape[0]
    pool_size = send_rows.shape[1]
    cap = pool_size // owners
    chips = owners // 2
    to_slab = slab_pairs(slabs, owners)

    def across(array):
        return lax.ppermute(array, "chaos", [(i, i ^ 1) for i in range(owners)])

    def plane(array, at):
        return lax.dynamic_index_in_dim(array, at, 1, keepdims=False)

    here, there = plane(field, core), plane(field, 1 - core)
    here_beside = across(there)
    send_rows, pick, mode_ids, coef, other, here_beside = lax.optimization_barrier(
        (send_rows, pick, mode_ids, coef, here, here_beside)
    )
    rows_beside, there_beside = across(send_rows), across(other)

    inside = jnp.where(core == 0, space > 0, space + 1 < slabs)
    flag = jnp.broadcast_to(inside.astype(jnp.int32), (1, field.shape[3]))

    rows = from_own(cap, send_rows), from_own(cap, rows_beside)
    def beside_chip(n):
        paired = (n > 0) & (n < chips // 2 * 2 - 1)
        return jnp.where(paired, jnp.where(n % 2 == 1, n + 1, n - 1), n)

    away = tuple(range(1, chips))
    turned = [n if n == 0 or n >= chips // 2 * 2 - 1 else n + 1 if n % 2 else n - 1 for n in range(chips)]
    to_chip = [[(i, i ^ (2 * (turned[n] if i % 2 else n))) for i in range(owners)] for n in range(chips)]
    def orders_of(emission):
        held = (chips - 1, *(emission.index(n) for n in away))
        return held, tuple(held[n] for n in turned)

    emission, emission_early = away[::-1], away
    orders = orders_of(emission)

    block = (pick // cap) ^ own
    step = jnp.where(core == 1, beside_chip(block // 2), block // 2)
    entry = (block % 2 * chips + step) * cap + pick % cap
    taken = entry[:, :, None] == jnp.arange(pool_size, dtype=jnp.int32)
    high = lax.reduce_precision(coef, 8, 7)
    place = jnp.concatenate(
        [jnp.where(taken, part[:, :, None], 0.0).astype(jnp.bfloat16) for part in (high, coef - high)], axis=2
    )
    which = (mode_ids[:, :, None] == jnp.arange(count_modes, dtype=jnp.int32)).astype(jnp.bfloat16)
    weights = jnp.einsum("isp,isk->kip", place, which, preferred_element_type=jnp.float32)
    weights = weights.reshape(count_modes * own_terms, 2 * pool_size)
    weights = weights[:, :pool_size] + weights[:, pool_size:]
    high = lax.reduce_precision(weights, 8, 7)
    weights = jnp.concatenate([high, weights - high], axis=1)
    weights = weights.astype(jnp.bfloat16), across(weights)
    mode_plane = plane(modes, core)

    def send(sent, kept, steps):
        return [lax.ppermute(sent[n - 1], "chaos", to_chip[n]) for n in steps] + [kept]

    def exchange(whole, centers, others):
        halos = [lax.ppermute(center, AXES, to_slab) for center in centers]
        inputs = (cap, rows, flag, local(centers, others, halos[:1]), halos[::-1])
        if whole:
            begun = images(1, True, (*away, 0), *inputs)
            sent = images(0, True, away, *inputs, begun[:-1])
            (kept,) = images(0, True, (0,), *inputs, begun[-1:], sent[-1:])
            return send(sent, kept, emission)
        pool, after = [], ()
        for a in (1, 0):
            sent = images(a, False, away, *inputs, (), after)
            (kept,) = images(a, False, (0,), *inputs, (), sent[-1:])
            pool.append(send(sent, kept, emission_early if a else emission))
            after = sent[-1:]
        return [*early(cap, orders_of(emission_early), pool[0]), *pool[1]]

    pool = exchange(True, (here, here_beside), (there, there_beside))
    own_first = product(0, cap, orders, weights[0], mode_plane, pool)
    first = own_first, product(1, cap, orders, weights[1], mode_plane, pool, (own_first,))
    beside = [across(x) for x in first]
    out, token = write(own_first, beside[1], True)
    pool = exchange(False, first, beside[::-1])
    theirs = across(product(1, cap, orders, weights[1], mode_plane, pool, (token,)))
    mine = product(0, cap, orders, weights[0], mode_plane, pool)
    return out, *write(mine, theirs, False)


def solution(mesh):
    slabs, owners = mesh.shape["space"], mesh.shape["chaos"]

    def per_device(*args):
        return body(slabs, owners, *args)

    in_specs = (
        P("chaos", "space", None, None),
        P(None, "space", None, None),
        P("chaos", None),
        P("chaos", None),
        P("chaos", None),
        P("chaos", None),
    )
    out_specs = (P("chaos", "space", None, None), P("chaos", "space", None, None))
    return jax.shard_map(
        per_device, mesh=mesh, in_specs=in_specs, out_specs=out_specs, check_vma=False
    )
```

```python
import functools

import jax
import jax.numpy as jnp
from jax import lax
from jax.experimental import pallas as pl
from jax.experimental.pallas import tpu as pltpu
from jax.sharding import PartitionSpec as P

AXES = ("space", "chaos")
ANY = pl.BlockSpec(memory_space=pl.ANY)
VMEM = pl.BlockSpec(memory_space=pltpu.VMEM)
BATCH = 8
PARAMS = pltpu.CompilerParams(vmem_limit_bytes=32 * 1024 * 1024)


def cost(flops):
    return pl.CostEstimate(flops=flops, bytes_accessed=1 << 20, transcendentals=0)


def slab_pairs(slabs, owners):
    pairs = []
    for s in range(slabs):
        for d in range(owners):
            beside = s + 1 if d % 2 else s - 1
            other = beside * owners + (d ^ 1) if 0 <= beside < slabs else s * owners + (d ^ 2 if owners > 2 else d)
            pairs.append((s * owners + d, other))
    return pairs


def local_kernel(center_own, center_beside, other_own, other_beside, *rest):
    gx, gy = center_own.shape[1:]
    sub = lax.broadcasted_iota(jnp.int32, (gx, gy), 0)
    lane = lax.broadcasted_iota(jnp.int32, (gx, gy), 1)
    zero = jnp.zeros((gx, gy), jnp.float32)

    def laplace(middle, other):
        beside = jnp.where(sub > 0, pltpu.roll(middle, 1, 0), zero)
        beside = beside + jnp.where(sub < gx - 1, pltpu.roll(middle, gx - 1, 0), zero)
        beside = beside + jnp.where(lane > 0, pltpu.roll(middle, 1, 1), zero)
        beside = beside + jnp.where(lane < gy - 1, pltpu.roll(middle, gy - 1, 1), zero)
        return 6.0 * middle - (beside + other)

    for center, other, out in zip((center_own, center_beside), (other_own, other_beside), rest[-2:]):
        for start in range(0, center.shape[0], BATCH):
            terms = range(start, min(start + BATCH, center.shape[0]))
            made = [laplace(center[term], other[term]) for term in terms]
            for term, value in zip(terms, made):
                out[term] = value


def local(centers, others, after=()):
    out = jax.ShapeDtypeStruct(centers[0].shape, jnp.float32)
    return pl.pallas_call(
        local_kernel,
        out_shape=[out, out],
        in_specs=[VMEM] * 4 + [ANY] * len(after),
        out_specs=[VMEM] * 2,
        compiler_params=PARAMS,
        cost_estimate=cost(out.size * 16),
        name="local",
    )(*centers, *others, *after)


def images_kernel(a, whole, chips, cap, rows, flag, partial, halo, *rest):
    outs = rest[-len(chips) :]
    gx, gy = partial.shape[1:]
    zero = jnp.zeros((gx, gy), jnp.float32)
    inside = flag[...] > 0
    terms = rows[...]
    for m, out in zip(chips, outs):
        for b in range(2):
            picked = [terms[0, (2 * m + b) * cap + c] for c in range(cap)]
            made = [partial[term] - jnp.where(inside, halo[term], zero) for term in picked]
            for c in range(cap):
                out[pl.ds((2 * b + a if whole else b) * gx * cap + c, gx, stride=cap), :] = made[c]


def images(a, whole, chips, cap, rows, flag, partial, halos, begun=(), after=()):
    gx, gy = partial[a].shape[1:]
    out = jax.ShapeDtypeStruct(((4 if whole else 2) * gx * cap, gy), jnp.float32)
    return pl.pallas_call(
        functools.partial(images_kernel, a, whole, chips, cap),
        out_shape=[out] * len(chips),
        in_specs=[VMEM] * (4 + len(begun)) + [ANY] * len(after),
        out_specs=[VMEM] * len(chips),
        input_output_aliases={4 + i: i for i in range(len(begun))},
        compiler_params=PARAMS,
        cost_estimate=cost(2 * gx * cap * gy * len(chips)),
        name=f"images_{a}_{chips[0]}",
    )(rows[a], flag, partial[a], halos[a], *begun, *after)


def halves_of(full):
    high = full.astype(jnp.bfloat16)
    return high, (full - high.astype(jnp.float32)).astype(jnp.bfloat16)


def early_kernel(cap, orders, *rest):
    arrays, (high, low) = rest[:-2], rest[-2:]
    gx = arrays[0].shape[0] // (2 * cap)
    count = len(arrays) * cap
    for b in range(2):
        for g in range(gx):
            n = b * gx + g
            full = jnp.concatenate([arrays[at][n * cap : (n + 1) * cap, :] for at in orders[b]], axis=0)
            high[n * count : (n + 1) * count, :], low[n * count : (n + 1) * count, :] = halves_of(full)


def early(cap, orders, arrays):
    rows, gy = arrays[0].shape
    out = jax.ShapeDtypeStruct((rows * len(arrays), gy), jnp.bfloat16)
    return pl.pallas_call(
        functools.partial(early_kernel, cap, orders),
        out_shape=[out, out],
        in_specs=[VMEM] * len(arrays),
        out_specs=[VMEM] * 2,
        compiler_params=PARAMS,
        cost_estimate=cost(1000),
        name="early",
    )(*arrays)


def product_kernel(b, cap, order, weights, modes, *rest):
    out = rest[-1]
    halves = weights[...].astype(jnp.bfloat16)
    both = jnp.concatenate([halves, halves], axis=1)
    count_modes, gx, gy = modes.shape
    own_terms = weights.shape[0] // count_modes
    count = len(order) * cap

    def blocks(arrays, n):
        return jnp.concatenate([arrays[at][n * cap : (n + 1) * cap, :] for at in order], axis=0)

    def column(g):
        if rest[0].dtype == jnp.bfloat16:
            n = b * gx + g
            late = halves_of(blocks(rest[2:], n))
            pairs = [(own, other[n * count : (n + 1) * count, :]) for own, other in zip(late, rest[:2])]
        else:
            owned = [halves_of(blocks(rest, (2 * b + a) * gx + g)) for a in range(2)]
            pairs = list(zip(*owned))
        parts = [part for pair in pairs for part in 2 * (pair[::-1] if b else pair)]
        return jnp.concatenate(parts, axis=0)

    for g in range(0, gx, 2):
        pool = jnp.concatenate([column(g), column(g + 1)], axis=1)
        mixed = jnp.dot(both, pool, preferred_element_type=jnp.float32)
        for side in range(2):
            total = jnp.zeros((own_terms, gy), jnp.float32)
            for k in range(count_modes):
                part = mixed[k * own_terms : (k + 1) * own_terms, side * gy : (side + 1) * gy]
                total = total + part * modes[k, pl.ds(g + side, 1), :]
            out[pl.ds(g + side, own_terms, stride=gx), :] = total


def product(b, cap, orders, weights, modes, pool, after=()):
    count_modes, gx, gy = modes.shape
    own_terms = weights.shape[0] // count_modes
    out = pl.pallas_call(
        functools.partial(product_kernel, b, cap, orders[b]),
        out_shape=jax.ShapeDtypeStruct((own_terms * gx, gy), jnp.float32),
        in_specs=[VMEM] * (2 + len(pool)) + [ANY] * len(after),
        out_specs=VMEM,
        compiler_params=PARAMS,
        cost_estimate=cost(4 * weights.shape[0] * weights.shape[1] * gx * gy),
        name=f"product_{b}",
    )(weights, modes, *pool, *after)
    return out.reshape(own_terms, gx, gy)


def write_kernel(here, there, out, *rest):
    sems = rest[-1]
    core = lax.rem(lax.axis_index("chaos"), 2)
    copies = [
        pltpu.make_async_copy(here, out.at[:, core], sems.at[0]),
        pltpu.make_async_copy(there, out.at[:, 1 - core], sems.at[1]),
    ]
    for copy in copies:
        copy.start()
    for token in rest[:-1]:
        token[...] = jnp.zeros_like(token)
    for copy in copies:
        copy.wait()


def write(here, there, token):
    terms, gx, gy = here.shape
    return pl.pallas_call(
        write_kernel,
        out_shape=[jax.ShapeDtypeStruct((terms, 2, gx, gy), jnp.float32)]
        + [jax.ShapeDtypeStruct((gx, gy), jnp.float32)] * token,
        in_specs=[VMEM] * 2,
        out_specs=[ANY] + [VMEM] * token,
        scratch_shapes=[pltpu.SemaphoreType.DMA((2,))],
        compiler_params=PARAMS,
        name="write",
    )(here, there)


def from_own_kernel(cap, listed, out):
    own = lax.axis_index("chaos")
    length, width = listed.shape[1], out.shape[1]
    row = listed[...]
    if width > length:
        row = jnp.concatenate([row, jnp.zeros((1, width - length), row.dtype)], axis=1)
    lane = lax.broadcasted_iota(jnp.int32, row.shape, 1)
    size = cap
    while size < length:
        turned = jnp.where(lane & size > 0, pltpu.roll(row, size, 1), pltpu.roll(row, width - size, 1))
        row = jnp.where((own & (size // cap)) > 0, turned, row)
        size *= 2
    chip = lane // (2 * cap)
    turned = jnp.where(chip % 2 == 1, pltpu.roll(row, width - 2 * cap, 1), pltpu.roll(row, 2 * cap, 1))
    moved = (chip > 0) & (chip < length // (2 * cap) // 2 * 2 - 1) & (own % 2 == 1)
    out[...] = jnp.where(moved, turned, row)


def from_own(cap, listed):
    width = -(-listed.shape[1] // 128) * 128
    return pl.pallas_call(
        functools.partial(from_own_kernel, cap),
        out_shape=jax.ShapeDtypeStruct((1, width), listed.dtype),
        in_specs=[VMEM],
        out_specs=VMEM,
        compiler_params=PARAMS,
        cost_estimate=cost(20_000_000_000),
        name="from_own",
    )(listed)


def body(slabs, owners, field, modes, send_rows, pick, mode_ids, coef):
    space, own = lax.axis_index("space"), lax.axis_index("chaos")
    core = own % 2
    own_terms = pick.shape[0]
    count_modes = modes.shape[0]
    pool_size = send_rows.shape[1]
    cap = pool_size // owners
    chips = owners // 2
    to_slab = slab_pairs(slabs, owners)

    def across(array):
        return lax.ppermute(array, "chaos", [(i, i ^ 1) for i in range(owners)])

    def plane(array, at):
        return lax.dynamic_index_in_dim(array, at, 1, keepdims=False)

    there = plane(field, 1 - core)
    field, there = lax.optimization_barrier((field, there))
    here = plane(field, core)
    here_beside = across(there)
    send_rows, pick, mode_ids, coef, other, here_beside = lax.optimization_barrier(
        (send_rows, pick, mode_ids, coef, here, here_beside)
    )
    rows_beside, there_beside = across(send_rows), across(other)

    inside = jnp.where(core == 0, space > 0, space + 1 < slabs)
    flag = jnp.broadcast_to(inside.astype(jnp.int32), (1, field.shape[3]))

    rows = from_own(cap, send_rows), from_own(cap, rows_beside)
    def beside_chip(n):
        paired = (n > 0) & (n < chips // 2 * 2 - 1)
        return jnp.where(paired, jnp.where(n % 2 == 1, n + 1, n - 1), n)

    away = tuple(range(1, chips))
    turned = [n if n == 0 or n >= chips // 2 * 2 - 1 else n + 1 if n % 2 else n - 1 for n in range(chips)]
    to_chip = [[(i, i ^ (2 * (turned[n] if i % 2 else n))) for i in range(owners)] for n in range(chips)]
    def orders_of(emission):
        held = (chips - 1, *(emission.index(n) for n in away))
        return held, tuple(held[n] for n in turned)

    emission, emission_early = away[::-1], away
    orders = orders_of(emission)

    block = (pick // cap) ^ own
    step = jnp.where(core == 1, beside_chip(block // 2), block // 2)
    entry = (block % 2 * chips + step) * cap + pick % cap
    taken = entry[:, :, None] == jnp.arange(pool_size, dtype=jnp.int32)
    high = lax.reduce_precision(coef, 8, 7)
    place = jnp.concatenate(
        [jnp.where(taken, part[:, :, None], 0.0).astype(jnp.bfloat16) for part in (high, coef - high)], axis=2
    )
    which = (mode_ids[:, :, None] == jnp.arange(count_modes, dtype=jnp.int32)).astype(jnp.bfloat16)
    weights = jnp.einsum("isp,isk->kip", place, which, preferred_element_type=jnp.float32)
    weights = weights.reshape(count_modes * own_terms, 2 * pool_size)
    weights = weights[:, :pool_size] + weights[:, pool_size:]
    high = lax.reduce_precision(weights, 8, 7)
    weights = jnp.concatenate([high, weights - high], axis=1)
    weights = weights.astype(jnp.bfloat16), across(weights)
    mode_plane = plane(modes, core)

    def send(sent, kept, steps):
        return [lax.ppermute(sent[n - 1], "chaos", to_chip[n]) for n in steps] + [kept]

    def exchange(whole, centers, others):
        halos = [lax.ppermute(center, AXES, to_slab) for center in centers]
        inputs = (cap, rows, flag, local(centers, others, halos[:1]), halos[::-1])
        if whole:
            begun = images(1, True, (*away, 0), *inputs)
            sent = images(0, True, away, *inputs, begun[:-1])
            (kept,) = images(0, True, (0,), *inputs, begun[-1:], sent[-1:])
            return send(sent, kept, emission)
        pool, after = [], ()
        for a in (1, 0):
            sent = images(a, False, away, *inputs, (), after)
            (kept,) = images(a, False, (0,), *inputs, (), sent[-1:])
            pool.append(send(sent, kept, emission_early if a else emission))
            after = sent[-1:]
        return [*early(cap, orders_of(emission_early), pool[0]), *pool[1]]

    pool = exchange(True, (here, here_beside), (there, there_beside))
    own_first = product(0, cap, orders, weights[0], mode_plane, pool)
    first = own_first, product(1, cap, orders, weights[1], mode_plane, pool, (own_first,))
    beside = [across(x) for x in first]
    out, token = write(own_first, beside[1], True)
    pool = exchange(False, first, beside[::-1])
    theirs = across(product(1, cap, orders, weights[1], mode_plane, pool, (token,)))
    mine = product(0, cap, orders, weights[0], mode_plane, pool)
    return out, *write(mine, theirs, False)


def solution(mesh):
    slabs, owners = mesh.shape["space"], mesh.shape["chaos"]

    def per_device(*args):
        return body(slabs, owners, *args)

    in_specs = (
        P("chaos", "space", None, None),
        P(None, "space", None, None),
        P("chaos", None),
        P("chaos", None),
        P("chaos", None),
        P("chaos", None),
    )
    out_specs = (P("chaos", "space", None, None), P("chaos", "space", None, None))
    return jax.shard_map(
        per_device, mesh=mesh, in_specs=in_specs, out_specs=out_specs, check_vma=False
    )
```

```python
import functools

import jax
import jax.numpy as jnp
from jax import lax
from jax.experimental import pallas as pl
from jax.experimental.pallas import tpu as pltpu
from jax.sharding import PartitionSpec as P

AXES = ("space", "chaos")
ANY = pl.BlockSpec(memory_space=pl.ANY)
VMEM = pl.BlockSpec(memory_space=pltpu.VMEM)
BATCH = 8
PARAMS = pltpu.CompilerParams(vmem_limit_bytes=32 * 1024 * 1024)


def cost(flops):
    return pl.CostEstimate(flops=flops, bytes_accessed=1 << 20, transcendentals=0)


def slab_pairs(slabs, owners):
    pairs = []
    for s in range(slabs):
        for d in range(owners):
            beside = s + 1 if d % 2 else s - 1
            other = beside * owners + (d ^ 1) if 0 <= beside < slabs else s * owners + (d ^ 2 if owners > 2 else d)
            pairs.append((s * owners + d, other))
    return pairs


def local_kernel(center, other, *rest):
    out = rest[-1]
    gx, gy = center.shape[1:]
    sub = lax.broadcasted_iota(jnp.int32, (gx, gy), 0)
    lane = lax.broadcasted_iota(jnp.int32, (gx, gy), 1)
    zero = jnp.zeros((gx, gy), jnp.float32)

    def laplace(middle, other):
        beside = jnp.where(sub > 0, pltpu.roll(middle, 1, 0), zero)
        beside = beside + jnp.where(sub < gx - 1, pltpu.roll(middle, gx - 1, 0), zero)
        beside = beside + jnp.where(lane > 0, pltpu.roll(middle, 1, 1), zero)
        beside = beside + jnp.where(lane < gy - 1, pltpu.roll(middle, gy - 1, 1), zero)
        return 6.0 * middle - (beside + other)

    for start in range(0, center.shape[0], BATCH):
        terms = range(start, min(start + BATCH, center.shape[0]))
        made = [laplace(center[term], other[term]) for term in terms]
        for term, value in zip(terms, made):
            out[term] = value


def local(a, center, other, *after):
    return pl.pallas_call(
        local_kernel,
        out_shape=jax.ShapeDtypeStruct(center.shape, jnp.float32),
        in_specs=[VMEM] * 2 + [ANY] * len(after),
        out_specs=VMEM,
        compiler_params=PARAMS,
        cost_estimate=cost(center.size * 8),
        name=f"local_{a}",
    )(center, other, *after)


def images_kernel(a, whole, chips, cap, rows, flag, partial, halo, *rest):
    outs = rest[-len(chips) :]
    gx, gy = partial.shape[1:]
    zero = jnp.zeros((gx, gy), jnp.float32)
    inside = flag[...] > 0
    terms = rows[...]
    for m, out in zip(chips, outs):
        for b in range(2):
            picked = [terms[0, (2 * m + b) * cap + c] for c in range(cap)]
            made = [partial[term] - jnp.where(inside, halo[term], zero) for term in picked]
            for c in range(cap):
                out[pl.ds((2 * b + a if whole else b) * gx * cap + c, gx, stride=cap), :] = made[c]


def images(a, whole, chips, cap, rows, flag, partial, halos, begun=(), after=()):
    gx, gy = partial[a].shape[1:]
    out = jax.ShapeDtypeStruct(((4 if whole else 2) * gx * cap, gy), jnp.float32)
    return pl.pallas_call(
        functools.partial(images_kernel, a, whole, chips, cap),
        out_shape=[out] * len(chips),
        in_specs=[VMEM] * (4 + len(begun)) + [ANY] * len(after),
        out_specs=[VMEM] * len(chips),
        input_output_aliases={4 + i: i for i in range(len(begun))},
        compiler_params=PARAMS,
        cost_estimate=cost(2 * gx * cap * gy * len(chips)),
        name=f"images_{a}_{chips[0]}",
    )(rows[a], flag, partial[a], halos[a], *begun, *after)


def halves_of(full):
    high = full.astype(jnp.bfloat16)
    return high, (full - high.astype(jnp.float32)).astype(jnp.bfloat16)


def early_kernel(cap, orders, *rest):
    arrays, (high, low) = rest[:-2], rest[-2:]
    gx = arrays[0].shape[0] // (2 * cap)
    count = len(arrays) * cap
    for b in range(2):
        for g in range(gx):
            n = b * gx + g
            full = jnp.concatenate([arrays[at][n * cap : (n + 1) * cap, :] for at in orders[b]], axis=0)
            high[n * count : (n + 1) * count, :], low[n * count : (n + 1) * count, :] = halves_of(full)


def early(cap, orders, arrays):
    rows, gy = arrays[0].shape
    out = jax.ShapeDtypeStruct((rows * len(arrays), gy), jnp.bfloat16)
    return pl.pallas_call(
        functools.partial(early_kernel, cap, orders),
        out_shape=[out, out],
        in_specs=[VMEM] * len(arrays),
        out_specs=[VMEM] * 2,
        compiler_params=PARAMS,
        cost_estimate=cost(1000),
        name="early",
    )(*arrays)


def product_kernel(b, cap, order, weights, modes, *rest):
    out = rest[-1]
    halves = weights[...].astype(jnp.bfloat16)
    both = jnp.concatenate([halves, halves], axis=1)
    count_modes, gx, gy = modes.shape
    own_terms = weights.shape[0] // count_modes
    count = len(order) * cap

    def blocks(arrays, n):
        return jnp.concatenate([arrays[at][n * cap : (n + 1) * cap, :] for at in order], axis=0)

    def column(g):
        if rest[0].dtype == jnp.bfloat16:
            n = b * gx + g
            late = halves_of(blocks(rest[2:], n))
            pairs = [(own, other[n * count : (n + 1) * count, :]) for own, other in zip(late, rest[:2])]
        else:
            owned = [halves_of(blocks(rest, (2 * b + a) * gx + g)) for a in range(2)]
            pairs = list(zip(*owned))
        parts = [part for pair in pairs for part in 2 * (pair[::-1] if b else pair)]
        return jnp.concatenate(parts, axis=0)

    for g in range(0, gx, 2):
        pool = jnp.concatenate([column(g), column(g + 1)], axis=1)
        mixed = jnp.dot(both, pool, preferred_element_type=jnp.float32)
        for side in range(2):
            total = jnp.zeros((own_terms, gy), jnp.float32)
            for k in range(count_modes):
                part = mixed[k * own_terms : (k + 1) * own_terms, side * gy : (side + 1) * gy]
                total = total + part * modes[k, pl.ds(g + side, 1), :]
            out[pl.ds(g + side, own_terms, stride=gx), :] = total


def product(b, cap, orders, weights, modes, pool, after=()):
    count_modes, gx, gy = modes.shape
    own_terms = weights.shape[0] // count_modes
    out = pl.pallas_call(
        functools.partial(product_kernel, b, cap, orders[b]),
        out_shape=jax.ShapeDtypeStruct((own_terms * gx, gy), jnp.float32),
        in_specs=[VMEM] * (2 + len(pool)) + [ANY] * len(after),
        out_specs=VMEM,
        compiler_params=PARAMS,
        cost_estimate=cost(4 * weights.shape[0] * weights.shape[1] * gx * gy),
        name=f"product_{b}",
    )(weights, modes, *pool, *after)
    return out.reshape(own_terms, gx, gy)


def write_kernel(here, there, out, *rest):
    sems = rest[-1]
    core = lax.rem(lax.axis_index("chaos"), 2)
    copies = [
        pltpu.make_async_copy(here, out.at[:, core], sems.at[0]),
        pltpu.make_async_copy(there, out.at[:, 1 - core], sems.at[1]),
    ]
    for copy in copies:
        copy.start()
    for token in rest[:-1]:
        token[...] = jnp.zeros_like(token)
    for copy in copies:
        copy.wait()


def write(here, there, token):
    terms, gx, gy = here.shape
    return pl.pallas_call(
        write_kernel,
        out_shape=[jax.ShapeDtypeStruct((terms, 2, gx, gy), jnp.float32)]
        + [jax.ShapeDtypeStruct((gx, gy), jnp.float32)] * token,
        in_specs=[VMEM] * 2,
        out_specs=[ANY] + [VMEM] * token,
        scratch_shapes=[pltpu.SemaphoreType.DMA((2,))],
        compiler_params=PARAMS,
        name="write",
    )(here, there)


def from_own_kernel(cap, listed, out):
    own = lax.axis_index("chaos")
    length, width = listed.shape[1], out.shape[1]
    row = listed[...]
    if width > length:
        row = jnp.concatenate([row, jnp.zeros((1, width - length), row.dtype)], axis=1)
    lane = lax.broadcasted_iota(jnp.int32, row.shape, 1)
    size = cap
    while size < length:
        turned = jnp.where(lane & size > 0, pltpu.roll(row, size, 1), pltpu.roll(row, width - size, 1))
        row = jnp.where((own & (size // cap)) > 0, turned, row)
        size *= 2
    chip = lane // (2 * cap)
    turned = jnp.where(chip % 2 == 1, pltpu.roll(row, width - 2 * cap, 1), pltpu.roll(row, 2 * cap, 1))
    moved = (chip > 0) & (chip < length // (2 * cap) // 2 * 2 - 1) & (own % 2 == 1)
    out[...] = jnp.where(moved, turned, row)


def from_own(cap, listed):
    width = -(-listed.shape[1] // 128) * 128
    return pl.pallas_call(
        functools.partial(from_own_kernel, cap),
        out_shape=jax.ShapeDtypeStruct((1, width), listed.dtype),
        in_specs=[VMEM],
        out_specs=VMEM,
        compiler_params=PARAMS,
        cost_estimate=cost(20_000_000_000),
        name="from_own",
    )(listed)


def body(slabs, owners, field, modes, send_rows, pick, mode_ids, coef):
    space, own = lax.axis_index("space"), lax.axis_index("chaos")
    core = own % 2
    own_terms = pick.shape[0]
    count_modes = modes.shape[0]
    pool_size = send_rows.shape[1]
    cap = pool_size // owners
    chips = owners // 2
    to_slab = slab_pairs(slabs, owners)

    def across(array):
        return lax.ppermute(array, "chaos", [(i, i ^ 1) for i in range(owners)])

    def plane(array, at):
        return lax.dynamic_index_in_dim(array, at, 1, keepdims=False)

    here, there = plane(field, core), plane(field, 1 - core)
    here_beside = across(there)
    send_rows, pick, mode_ids, coef, other, here_beside = lax.optimization_barrier(
        (send_rows, pick, mode_ids, coef, here, here_beside)
    )
    rows_beside, there_beside = across(send_rows), across(other)

    inside = jnp.where(core == 0, space > 0, space + 1 < slabs)
    flag = jnp.broadcast_to(inside.astype(jnp.int32), (1, field.shape[3]))

    rows = from_own(cap, send_rows), from_own(cap, rows_beside)
    def beside_chip(n):
        paired = (n > 0) & (n < chips // 2 * 2 - 1)
        return jnp.where(paired, jnp.where(n % 2 == 1, n + 1, n - 1), n)

    away = tuple(range(1, chips))
    turned = [n if n == 0 or n >= chips // 2 * 2 - 1 else n + 1 if n % 2 else n - 1 for n in range(chips)]
    to_chip = [[(i, i ^ (2 * (turned[n] if i % 2 else n))) for i in range(owners)] for n in range(chips)]
    def orders_of(emission):
        held = (chips - 1, *(emission.index(n) for n in away))
        return held, tuple(held[n] for n in turned)

    emission, emission_early = away[::-1], away
    orders = orders_of(emission)

    block = (pick // cap) ^ own
    step = jnp.where(core == 1, beside_chip(block // 2), block // 2)
    entry = (block % 2 * chips + step) * cap + pick % cap
    taken = entry[:, :, None] == jnp.arange(pool_size, dtype=jnp.int32)
    high = lax.reduce_precision(coef, 8, 7)
    place = jnp.concatenate(
        [jnp.where(taken, part[:, :, None], 0.0).astype(jnp.bfloat16) for part in (high, coef - high)], axis=2
    )
    which = (mode_ids[:, :, None] == jnp.arange(count_modes, dtype=jnp.int32)).astype(jnp.bfloat16)
    weights = jnp.einsum("isp,isk->kip", place, which, preferred_element_type=jnp.float32)
    weights = weights.reshape(count_modes * own_terms, 2 * pool_size)
    weights = weights[:, :pool_size] + weights[:, pool_size:]
    high = lax.reduce_precision(weights, 8, 7)
    weights = jnp.concatenate([high, weights - high], axis=1)
    weights = weights.astype(jnp.bfloat16), across(weights)
    mode_plane = plane(modes, core)

    def send(sent, kept, steps):
        return [lax.ppermute(sent[n - 1], "chaos", to_chip[n]) for n in steps] + [kept]

    def exchange(whole, centers, others):
        halos = [lax.ppermute(center, AXES, to_slab) for center in centers]
        partial = [None, local(1, centers[1], others[1], halos[0])]
        inputs = (cap, rows, flag, partial, halos[::-1])
        if whole:
            partial[0] = local(0, centers[0], others[0], halos[0])
            begun = images(1, True, (*away, 0), *inputs)
            sent = images(0, True, away, *inputs, begun[:-1])
            (kept,) = images(0, True, (0,), *inputs, begun[-1:], sent[:1])
            return send(sent, kept, emission)
        pool, after = [], ()
        for a in (1, 0):
            sent = images(a, False, away, *inputs, (), after)
            (kept,) = images(a, False, (0,), *inputs, (), sent[-1:] if a else sent[:1])
            pool.append(send(sent, kept, emission_early if a else emission))
            after = sent[-1:]
            partial[0] = local(0, centers[0], others[0], sent[-1])
        return [*early(cap, orders_of(emission_early), pool[0]), *pool[1]]

    pool = exchange(True, (here, here_beside), (there, there_beside))
    own_first = product(0, cap, orders, weights[0], mode_plane, pool)
    first = own_first, product(1, cap, orders, weights[1], mode_plane, pool, (own_first,))
    beside = [across(x) for x in first]
    out, token = write(own_first, beside[1], True)
    pool = exchange(False, first, beside[::-1])
    theirs = across(product(1, cap, orders, weights[1], mode_plane, pool, (token,)))
    mine = product(0, cap, orders, weights[0], mode_plane, pool)
    return out, *write(mine, theirs, False)


def solution(mesh):
    slabs, owners = mesh.shape["space"], mesh.shape["chaos"]

    def per_device(*args):
        return body(slabs, owners, *args)

    in_specs = (
        P("chaos", "space", None, None),
        P(None, "space", None, None),
        P("chaos", None),
        P("chaos", None),
        P("chaos", None),
        P("chaos", None),
    )
    out_specs = (P("chaos", "space", None, None), P("chaos", "space", None, None))
    return jax.shard_map(
        per_device, mesh=mesh, in_specs=in_specs, out_specs=out_specs, check_vma=False
    )
```
